128 devices in a mesh: ctx: 8 (over z, x_hi), tp: 16 (over y, x_lo, core).
Axes of the slice: x: 4 (x_hi: 2, x_lo: 2; x = x_hi * 2 + x_lo), y: 4, z: 4, core: 2. Of those that a mesh axis runs over, the one named last changes fastest.
Arguments:
- prompt_queries: bfloat16 [4096, 16384], P('ctx', 'tp'), may hold values from -10 to 10
- prompt_keys: bfloat16 [4096, 1024], P('ctx', 'tp'), may hold values from -10 to 10
- prompt_values: bfloat16 [4096, 1024], P('ctx', 'tp'), may hold values from -6 to 6
- block_slot: int32 [32], replicated, may hold values from 0 to 31, each once
- decode_queries: bfloat16 [512, 16384], P('ctx', 'tp'), may hold values from -10 to 10
- new_keys: bfloat16 [512, 1024], P('ctx', 'tp'), may hold values from -6 to 6
- new_values: bfloat16 [512, 1024], P('ctx', 'tp'), may hold values from -6 to 6
- key_pool: bfloat16 [2048, 128, 1024], P(('ctx', 'tp')), may hold values from -10 to 10
- value_pool: bfloat16 [2048, 128, 1024], P(('ctx', 'tp')), may hold values from -6 to 6
- slot_map: int32 [512, 4], P(('ctx', 'tp')), may hold values from 0 to 15, as said below
- cache_lengths: int32 [512], P(('ctx', 'tp')), may hold values from 2 to 512, as said below
Outputs:
- prompt_out: bfloat16 [4096, 16384], P('ctx', 'tp')
- relaid_keys: bfloat16 [32, 128, 1024], P('ctx', None, 'tp')
- relaid_values: bfloat16 [32, 128, 1024], P('ctx', None, 'tp')
- decode_out: bfloat16 [512, 16384], P('ctx', 'tp')
The draws below stay inside these ranges and needn't reach their ends.
Inputs may be any that keep to these rules, and one draw needn't show every extreme that they name: `slot_map`: within the 4 rows of one device the 16 entries are all different. `cache_lengths`: on every device some row has exactly 512 cached tokens.
All inputs are finite; a program needn't handle non-finite values.
Results may differ from the reference program's by a relative error of at most 0.006.
Values may be sent and summed in bfloat16 or wider, within the bound.
A program may use at most 128 MiB of HBM per device.

```python
import math
import jax
import jax.numpy as jnp
from jax import lax

QHEADS = 128
KVHEADS = 8
HEAD_DIM = 128
PAGE = 128
ROWS_DEV = 4
MAX_BLOCKS = 4
PROMPT = 4096
BLOCKS = 32
MAX_LEN = 512
POOL_DEV = 16
ROWS = 512
POOL = 2048


def slot_helper(key):
    base = jax.random.fold_in(key, 303)
    groups = ROWS // ROWS_DEV
    keys = jax.random.split(base, groups)
    perms = jax.vmap(lambda one: jax.random.permutation(one, POOL_DEV))(keys)
    return perms.reshape(ROWS, MAX_BLOCKS).astype(jnp.int32)


def draw_prompt_queries(key, part):
    key = jax.random.fold_in(key, 1)
    base = jax.random.truncated_normal(key, -4.0, 4.0, (PROMPT, QHEADS * HEAD_DIM)).astype(jnp.float32)
    return base.astype(jnp.bfloat16)


def draw_prompt_keys(key, part):
    key = jax.random.fold_in(key, 2)
    base = jax.random.truncated_normal(key, -4.0, 4.0, (PROMPT, KVHEADS, HEAD_DIM)).astype(jnp.float32)
    return base.reshape(PROMPT, KVHEADS * HEAD_DIM).astype(jnp.bfloat16)


def draw_decode_queries(key, part):
    key = jax.random.fold_in(key, 3)
    base = jax.random.truncated_normal(key, -4.0, 4.0, (ROWS, QHEADS * HEAD_DIM)).astype(jnp.float32)
    return base.astype(jnp.bfloat16)


def draw_key_pool(key, part):
    key = jax.random.fold_in(key, 4)
    base = jax.random.truncated_normal(key, -4.0, 4.0, (POOL, PAGE, KVHEADS, HEAD_DIM)).astype(jnp.float32)
    return base.reshape(POOL, PAGE, KVHEADS * HEAD_DIM).astype(jnp.bfloat16)


def draw_slot_map(key, part):
    return slot_helper(key)


def draw_cache_lengths(key, part):
    key = jax.random.fold_in(key, 5)
    first, second = jax.random.split(key)
    lengths = jax.random.randint(first, (ROWS // ROWS_DEV, ROWS_DEV), 2, MAX_LEN + 1)
    chosen = jax.random.randint(second, (ROWS // ROWS_DEV, 1), 0, ROWS_DEV)
    lengths = jnp.where(jnp.arange(ROWS_DEV, dtype=jnp.int32)[None, :] == chosen, MAX_LEN, lengths)
    return lengths.reshape(ROWS).astype(jnp.int32)


def block_scale(own_key, extent, pieces, least, largest):
    loudness = 1.0
    for position, parts in pieces:
        steps = jax.random.uniform(jax.random.fold_in(jax.random.fold_in(own_key, 6), position), (parts,), jnp.float32, least / len(pieces), largest / len(pieces))
        loudness = loudness * jnp.repeat(jnp.exp(steps), extent[position] // parts).reshape((-1,) + (1,) * (len(extent) - 1 - position))
    return loudness


def bell_draw(rng, extent, scale, reach, cuts=(), kind=jnp.bfloat16):
    array = jax.random.normal(rng, extent, jnp.float32) * scale
    if len(cuts) > 0:
        array = block_scale(rng, extent, cuts, -0.22, 0.18) * array
    return jnp.clip(array, min=-reach, max=reach).astype(kind)


def setup_inputs(seed: int = 0) -> dict:
    seeds = jax.random.split(jax.random.key(seed), 12)
    prompt_queries = draw_prompt_queries(jax.random.fold_in(seeds[11], 71), 0)
    prompt_keys = draw_prompt_keys(jax.random.fold_in(seeds[11], 71), 0)
    prompt_values = bell_draw(seeds[2], (PROMPT, KVHEADS * HEAD_DIM), 1.0, 6.0, ((0, 8), (1, 16)))
    block_slot = jax.random.permutation(seeds[3], BLOCKS).astype(jnp.int32)
    decode_queries = draw_decode_queries(jax.random.fold_in(seeds[11], 71), 0)
    new_keys = bell_draw(seeds[5], (ROWS, KVHEADS * HEAD_DIM), 1.0, 6.0, ((0, 8), (1, 16)))
    new_values = bell_draw(seeds[6], (ROWS, KVHEADS * HEAD_DIM), 1.0, 6.0, ((0, 8), (1, 16)))
    key_pool = draw_key_pool(jax.random.fold_in(seeds[11], 71), 0)
    value_pool = bell_draw(seeds[8], (POOL, PAGE, KVHEADS * HEAD_DIM), 1.0, 6.0, ((0, 128),))
    slot_map = draw_slot_map(jax.random.fold_in(seeds[11], 71), 0)
    cache_lengths = draw_cache_lengths(jax.random.fold_in(seeds[11], 71), 0)
    return dict(prompt_queries=prompt_queries, prompt_keys=prompt_keys, prompt_values=prompt_values, block_slot=block_slot, decode_queries=decode_queries, new_keys=new_keys, new_values=new_values, key_pool=key_pool, value_pool=value_pool, slot_map=slot_map, cache_lengths=cache_lengths)


def prefill_head(head, prompt_queries, prompt_keys, prompt_values):
    group = head // (QHEADS // KVHEADS)
    query = lax.dynamic_slice_in_dim(prompt_queries, head * HEAD_DIM, HEAD_DIM, 1)
    key_head = lax.dynamic_slice_in_dim(prompt_keys, group * HEAD_DIM, HEAD_DIM, 1)
    value_head = lax.dynamic_slice_in_dim(prompt_values, group * HEAD_DIM, HEAD_DIM, 1)
    scores = jnp.dot(query, key_head.T, preferred_element_type=jnp.float32) * (1.0 / math.sqrt(HEAD_DIM))
    positions = jnp.arange(PROMPT, dtype=jnp.int32)
    causal = positions[None, :] <= positions[:, None]
    peak = lax.optimization_barrier(jnp.max(jnp.where(causal, scores, -1e+30), axis=1, keepdims=True))
    weights = jnp.where(causal, jnp.exp(scores - peak), 0.0)
    totals = lax.optimization_barrier(jnp.sum(weights, axis=1, keepdims=True))
    mixed = jnp.dot(weights.astype(jnp.bfloat16), value_head, preferred_element_type=jnp.float32)
    return (mixed / totals).astype(jnp.bfloat16)

def decode_row(items, key_pool, value_pool):
    query_row, key_new, value_new, slots, length, row = items
    pages = row // ROWS_DEV * POOL_DEV + slots
    cached_keys = key_pool[pages].reshape(MAX_LEN, KVHEADS, HEAD_DIM).astype(jnp.float32)
    cached_values = value_pool[pages].reshape(MAX_LEN, KVHEADS, HEAD_DIM).astype(jnp.float32)
    query = query_row.reshape(KVHEADS, QHEADS // KVHEADS, HEAD_DIM).astype(jnp.float32)
    scale = 1.0 / math.sqrt(HEAD_DIM)
    scores = jnp.einsum('kgd,tkd->kgt', query, cached_keys) * scale
    own = jnp.einsum('kgd,kd->kg', query, key_new.reshape(KVHEADS, HEAD_DIM).astype(jnp.float32)) * scale
    valid = (jnp.arange(MAX_LEN, dtype=jnp.int32) < length)[None, None, :]
    peak = jnp.maximum(lax.optimization_barrier(jnp.max(jnp.where(valid, scores, -1e+30), axis=-1)), own)
    weights = jnp.where(valid, jnp.exp(scores - peak[..., None]), 0.0)
    own_weight = jnp.exp(own - peak)
    total = lax.optimization_barrier(jnp.sum(weights, axis=-1)) + own_weight
    mixed = jnp.einsum('kgt,tkd->kgd', weights.astype(jnp.bfloat16).astype(jnp.float32), cached_values)
    own_value = value_new.reshape(KVHEADS, 1, HEAD_DIM).astype(jnp.float32)
    mixed = mixed + own_weight.astype(jnp.bfloat16).astype(jnp.float32)[..., None] * own_value
    return (mixed / total[..., None]).reshape(QHEADS * HEAD_DIM).astype(jnp.bfloat16)

def reference(prompt_queries, prompt_keys, prompt_values, block_slot, decode_queries, new_keys, new_values, key_pool, value_pool, slot_map, cache_lengths):
    heads_out = lax.map(lambda head: prefill_head(head, prompt_queries, prompt_keys, prompt_values), jnp.arange(QHEADS, dtype=jnp.int32))
    prompt_out = jnp.transpose(heads_out, (1, 0, 2)).reshape(PROMPT, QHEADS * HEAD_DIM)
    key_blocks = prompt_keys.reshape(BLOCKS, PAGE, KVHEADS * HEAD_DIM)
    value_blocks = prompt_values.reshape(BLOCKS, PAGE, KVHEADS * HEAD_DIM)
    relaid_keys = jnp.zeros_like(key_blocks).at[block_slot].set(key_blocks)
    relaid_values = jnp.zeros_like(value_blocks).at[block_slot].set(value_blocks)
    rows = jnp.arange(ROWS, dtype=jnp.int32)
    decode_out = lax.map(lambda items: decode_row(items, key_pool, value_pool), (decode_queries, new_keys, new_values, slot_map, cache_lengths, rows))
    return (prompt_out, relaid_keys, relaid_values, decode_out)
```

```python
import functools
import math

import jax
import jax.numpy as jnp
from jax import lax
from jax.experimental import pallas as pl
from jax.experimental.pallas import tpu as pltpu
from jax.sharding import PartitionSpec as P

HEAD = 128
PAGE = 128
CTX = 8
TP = 16
SEQ = 512
HEADS = 8
GROUPS = 8
ROWS = 4
SPAN = 2048
MSG = 48
F32 = jnp.float32
BF16 = jnp.bfloat16
MESH = pl.DeviceIdType.MESH
LOW = -1e30
SCALE = math.log2(math.e) / math.sqrt(HEAD)


def split_scaled(x):
    x = x.astype(F32) * SCALE
    high = x.astype(BF16)
    low = (x - high.astype(F32)).astype(BF16)
    return jnp.concatenate([high, low], axis=1)


def kernel(
    pq_ref, kt_ref, vt_ref, dq_ref, nk_ref, nv_ref, kp_ref, vp_ref, slots_ref, lens_ref, place_ref,
    out_ref, rk_ref, rv_ref, dout_ref,
    pq, qs, kv, vn, m_s, l_s, acc_s, kpool, vpool, bias, dsend, drecv, rsend, rrecv,
    local_sem, kv_ssem, kv_rsem, fw_ssem, fw_rsem, d_ssem, d_rsem, r_ssem, r_rsem,
):
    me = lax.axis_index("ctx")
    tp = lax.axis_index("tp")
    core = tp % 2
    mate = tp + 1 - 2 * core

    barrier = pltpu.get_barrier_semaphore()
    for d in range(1, CTX):
        pl.semaphore_signal(barrier, inc=1, device_id=((me + d) % CTX, tp), device_id_type=MESH)
    for d in range(1, TP):
        pl.semaphore_signal(barrier, inc=1, device_id=(me, (tp + d) % TP), device_id_type=MESH)

    load_q = pltpu.make_async_copy(pq_ref, pq, local_sem.at[0])
    load_k = pltpu.make_async_copy(kp_ref, kpool, local_sem.at[1])
    load_v = pltpu.make_async_copy(vp_ref, vpool, local_sem.at[2])
    load_q.start()
    load_k.start()
    load_v.start()

    half = pl.ds(pl.multiple_of(core * 64, 64), 64)

    def tokens(block):
        return pl.ds(pl.multiple_of(block * SEQ, SEQ), SEQ)

    kv[0, half, tokens(me)] = kt_ref[...]
    kv[1, half, tokens(me)] = vt_ref[...]

    sub = lax.broadcasted_iota(jnp.int32, (8, HEAD), 0)
    lane = lax.broadcasted_iota(jnp.int32, (8, HEAD), 1)
    first_rows = sub < 4
    for p in range(4):
        x16 = dq_ref[16 * p : 16 * p + 16, :].astype(F32)
        n16 = jnp.concatenate(
            [nk_ref[16 * p : 16 * p + 16, :], nv_ref[16 * p : 16 * p + 16, :]], axis=1
        ).astype(F32)
        for o in range(2):
            x = x16[8 * o : 8 * o + 8]
            n = n16[8 * o : 8 * o + 8]
            even, odd = [], []
            for i in range(4):
                a = x[:, 2 * i * HEAD : (2 * i + 1) * HEAD]
                b = x[:, (2 * i + 1) * HEAD : (2 * i + 2) * HEAD]
                even.append(jnp.where(first_rows, a, pltpu.roll(b, 4, 0)))
                odd.append(jnp.where(first_rows, pltpu.roll(a, 4, 0), b))
            turned = pltpu.roll(n, 4, 0)
            dsend[4 * p + 2 * o] = jnp.concatenate(even + [n, n], axis=0).astype(BF16)
            dsend[4 * p + 2 * o + 1] = jnp.concatenate(odd + [turned, turned], axis=0).astype(BF16)
    drecv[tp] = dsend[tp]

    pl.semaphore_wait(barrier, CTX + TP - 2)

    def push(block, ctx):
        return pltpu.make_async_remote_copy(
            src_ref=kv.at[:, half, tokens(block)],
            dst_ref=kv.at[:, half, tokens(block)],
            send_sem=kv_ssem.at[ctx],
            recv_sem=kv_rsem.at[block],
            device_id=(ctx, tp),
            device_id_type=MESH,
        )

    def forward(block):
        return pltpu.make_async_remote_copy(
            src_ref=kv.at[:, half, tokens(block)],
            dst_ref=kv.at[:, half, tokens(block)],
            send_sem=fw_ssem.at[block],
            recv_sem=fw_rsem.at[block],
            device_id=(me, mate),
            device_id_type=MESH,
        )

    def ask(other, slot):
        return pltpu.make_async_remote_copy(
            src_ref=dsend.at[other],
            dst_ref=drecv.at[slot],
            send_sem=d_ssem.at[other],
            recv_sem=d_rsem.at[slot],
            device_id=(me, other),
            device_id_type=MESH,
        )

    def answer(other, slot):
        return pltpu.make_async_remote_copy(
            src_ref=rsend.at[other],
            dst_ref=rrecv.at[slot],
            send_sem=r_ssem.at[other],
            recv_sem=r_rsem.at[slot],
            device_id=(me, other),
            device_id_type=MESH,
        )

    def others(do):
        def body(d, carry):
            do((tp + d) % TP)
            return carry

        lax.fori_loop(1, TP, body, 0)

    forward(me).start()
    others(lambda other: ask(other, tp).start())
    for d in range(1, CTX):
        push(me, me ^ d).start()

    token = lax.broadcasted_iota(jnp.int32, (8, SPAN), 1)
    row = lax.broadcasted_iota(jnp.int32, (8, SPAN), 0) % ROWS
    visible = jnp.zeros((8, SPAN), F32)
    for r in range(ROWS):
        for b in range(4):
            left = jnp.minimum(lens_ref[r] - b * PAGE, PAGE)
            start = slots_ref[r, b] * PAGE
            inside = (token >= start) & (token < start + left) & (row == r)
            visible = jnp.where(inside, 1.0, visible)
    bias[...] = jnp.where(visible > 0.5, 0.0, LOW)

    load_q.wait()
    for h in range(HEADS):
        qs[h] = split_scaled(pq[:, h * HEAD : (h + 1) * HEAD])

    def turn(block):
        vn[tokens(block), :] = kv[1, :, tokens(block)].T

    def unit(h, block, count, diagonal):
        width = count * SEQ
        where = pl.ds(pl.multiple_of(block * SEQ, SEQ), width)
        keys = kv[0, :, where]
        s = jnp.dot(qs[h], jnp.concatenate([keys, keys], axis=0), preferred_element_type=F32)
        if diagonal:
            query = lax.broadcasted_iota(jnp.int32, s.shape, 0)
            key = lax.broadcasted_iota(jnp.int32, s.shape, 1)
            s = jnp.where(key <= query, s, LOW)
        peak = jnp.max(s, axis=1, keepdims=True)
        if diagonal:
            peak = jnp.broadcast_to(peak, (SEQ, HEAD))
        else:
            before = m_s[h]
            peak = jnp.maximum(before, peak)
            factor = jnp.exp2(before - peak)
        m_s[h] = peak
        probs, total = [], None
        for g in range(width // HEAD):
            p = jnp.exp2(s[:, g * HEAD : (g + 1) * HEAD] - peak)
            total = p if total is None else total + p
            probs.append(p.astype(BF16))
        mixed = jnp.dot(jnp.concatenate(probs, axis=1), vn[where, :], preferred_element_type=F32)
        if diagonal:
            l_s[h] = total
            acc_s[h] = mixed
        else:
            l_s[h] = l_s[h] * factor + total
            acc_s[h] = acc_s[h] * factor + mixed

    def heads(block, count, diagonal=False):
        def body(i, carry):
            unit(2 * i, block, count, diagonal)
            unit(2 * i + 1, block, count, diagonal)
            return carry

        lax.fori_loop(0, HEADS // 2, body, 0)

    def take(block):
        push(block, me).wait_recv()
        forward(block).start()

    forward(me).wait_recv()
    turn(me)
    heads(me, 1, diagonal=True)

    others(lambda other: ask(other, other).wait_recv())
    load_k.wait()
    load_v.wait()

    def decode_head(g):
        columns = pl.ds(pl.multiple_of(g * HEAD, HEAD), HEAD)
        mine, next_ = drecv[2 * g], drecv[2 * g + 1]
        q = jnp.concatenate([mine[:32], next_[:32]], axis=0)
        a, b = mine[32:48].astype(F32)[:8], next_[32:48].astype(F32)[:8]
        left = lane < 64
        new_k = jnp.where(left, a, pltpu.roll(b, 64, 1))
        new_v = jnp.where(left, pltpu.roll(a, 64, 1), b)
        new_k = jnp.where(first_rows, new_k, pltpu.roll(new_k, 4, 0))
        new_v = jnp.where(first_rows, new_v, pltpu.roll(new_v, 4, 0))
        s = lax.dot_general(
            q, kpool[:, columns], (((1,), (1,)), ((), ())), preferred_element_type=F32
        )
        s = (s * SCALE).reshape(8, 8, SPAN) + bias[...][None]
        own = jnp.sum(q.astype(F32).reshape(8, 8, HEAD) * new_k[None], axis=2, keepdims=True)
        own = own * SCALE
        peak = jnp.maximum(jnp.max(s, axis=2, keepdims=True), own)
        p = jnp.exp2(s - peak)
        own = jnp.exp2(own - peak)
        total = jnp.sum(p, axis=2, keepdims=True) + own
        mixed = jnp.dot(
            p.reshape(64, SPAN).astype(BF16), vpool[:, columns], preferred_element_type=F32
        ).reshape(8, 8, HEAD)
        mixed = mixed + own.astype(BF16).astype(F32) * new_v[None]
        result = (mixed / total).reshape(64, HEAD).astype(BF16)
        rsend[2 * g] = result[:32]
        rsend[2 * g + 1] = result[32:]

    def decode_two(i, carry):
        decode_head(2 * i)
        decode_head(2 * i + 1)
        return carry

    lax.fori_loop(0, GROUPS // 2, decode_two, 0)
    rrecv[tp] = rsend[tp]
    others(lambda other: answer(other, tp).start())

    take(me ^ 1)
    take(me ^ 2)
    take(me ^ 3)

    def full(block):
        forward(block).wait_recv()
        turn(block)

    full(me ^ 1)

    @pl.when(me % 2 == 1)
    def _():
        heads(me - 1, 1)

    full(me ^ 2)
    full(me ^ 3)
    for d in range(4, CTX):
        take(me ^ d)

    @pl.when(me // 2 % 2 == 1)
    def _():
        heads(me // 4 * 4, 2)

    for d in range(4, CTX):
        full(me ^ d)

    @pl.when(me // 4 == 1)
    def _():
        heads(0, 4)

    for h in range(HEADS):
        total = jnp.sum(l_s[h], axis=1, keepdims=True)
        out_ref[:, h * HEAD : (h + 1) * HEAD] = (acc_s[h] / total).astype(BF16)

    def relay(b, slots):
        columns = pl.ds(pl.multiple_of(b * PAGE, PAGE), PAGE)
        block = kv[:, half, columns].reshape(8, 16, PAGE)
        given = []
        for i in range(4):
            chosen = jnp.where(place_ref[b] == me * 4 + i, 1.0, 0.0)
            given.append(slots[i] + block * jnp.full((1, 16, PAGE), chosen, F32).astype(BF16))
        return tuple(given)

    empty = jnp.zeros((8, 16, PAGE), BF16)
    for i, slot in enumerate(lax.fori_loop(0, CTX * 4, relay, (empty,) * 4)):
        slot = slot.reshape(2, 64, PAGE)
        rk_ref[i] = slot[0]
        rv_ref[i] = slot[1]

    others(lambda other: answer(other, other).wait_recv())
    for p in range(4):
        pieces = []
        for o in range(2):
            even = rrecv[4 * p + 2 * o].astype(F32)
            odd = rrecv[4 * p + 2 * o + 1].astype(F32)
            columns = []
            for i in range(4):
                a, b = even[8 * i : 8 * i + 8], odd[8 * i : 8 * i + 8]
                columns.append(jnp.where(first_rows, a, pltpu.roll(b, 4, 0)))
                columns.append(jnp.where(first_rows, pltpu.roll(a, 4, 0), b))
            pieces.append(jnp.concatenate(columns, axis=1))
        dout_ref[16 * p : 16 * p + 16, :] = jnp.concatenate(pieces, axis=0).astype(BF16)

    for d in range(1, CTX):
        push(me, me ^ d).wait_send()
    for d in range(CTX):
        forward(me ^ d).wait_send()
    others(lambda other: ask(other, tp).wait_send())
    others(lambda other: answer(other, tp).wait_send())


def shards(
    prompt_queries,
    prompt_keys,
    prompt_values,
    block_slot,
    decode_queries,
    new_keys,
    new_values,
    key_pool,
    value_pool,
    slot_map,
    cache_lengths,
):
    vmem = pl.BlockSpec(memory_space=pltpu.VMEM)
    smem = pl.BlockSpec(memory_space=pltpu.SMEM)
    hbm = pl.BlockSpec(memory_space=pl.ANY)
    state = pltpu.VMEM((HEADS, SEQ, HEAD), F32)
    dma = pltpu.SemaphoreType.DMA
    prompt_out, relaid_keys, relaid_values, decode_out = pl.pallas_call(
        kernel,
        out_shape=(
            jax.ShapeDtypeStruct((SEQ, HEADS * HEAD), BF16),
            jax.ShapeDtypeStruct((4, 64, PAGE), BF16),
            jax.ShapeDtypeStruct((4, 64, PAGE), BF16),
            jax.ShapeDtypeStruct((64, HEADS * HEAD), BF16),
        ),
        in_specs=[hbm, vmem, vmem, vmem, vmem, vmem, hbm, hbm, smem, smem, smem],
        out_specs=(vmem, vmem, vmem, vmem),
        scratch_shapes=[
            pltpu.VMEM((SEQ, HEADS * HEAD), BF16),
            pltpu.VMEM((HEADS, SEQ, 2 * HEAD), BF16),
            pltpu.VMEM((2, HEAD, CTX * SEQ), BF16),
            pltpu.VMEM((CTX * SEQ, HEAD), BF16),
            state,
            state,
            state,
            pltpu.VMEM((SPAN, GROUPS * HEAD), BF16),
            pltpu.VMEM((SPAN, GROUPS * HEAD), BF16),
            pltpu.VMEM((8, SPAN), F32),
            pltpu.VMEM((TP, MSG, HEAD), BF16),
            pltpu.VMEM((TP, MSG, HEAD), BF16),
            pltpu.VMEM((TP, 32, HEAD), BF16),
            pltpu.VMEM((TP, 32, HEAD), BF16),
            dma((3,)),
            dma((CTX,)),
            dma((CTX,)),
            dma((CTX,)),
            dma((CTX,)),
            dma((TP,)),
            dma((TP,)),
            dma((TP,)),
            dma((TP,)),
        ],
        compiler_params=pltpu.CompilerParams(
            collective_id=0, has_side_effects=True, vmem_limit_bytes=60 * 2**20
        ),
    )(
        prompt_queries,
        prompt_keys.T,
        prompt_values.T,
        decode_queries,
        new_keys,
        new_values,
        key_pool.reshape(SPAN, GROUPS * HEAD),
        value_pool.reshape(SPAN, GROUPS * HEAD),
        slot_map,
        cache_lengths,
        block_slot,
    )
    return (
        prompt_out,
        jnp.swapaxes(relaid_keys, 1, 2),
        jnp.swapaxes(relaid_values, 1, 2),
        decode_out,
    )


def solution(mesh):
    return jax.shard_map(
        shards,
        mesh=mesh,
        in_specs=(
            P("ctx", "tp"),
            P("ctx", "tp"),
            P("ctx", "tp"),
            P(),
            P("ctx", "tp"),
            P("ctx", "tp"),
            P("ctx", "tp"),
            P(("ctx", "tp"), None, None),
            P(("ctx", "tp"), None, None),
            P(("ctx", "tp"), None),
            P(("ctx", "tp")),
        ),
        out_specs=(P("ctx", "tp"), P("ctx", None, "tp"), P("ctx", None, "tp"), P("ctx", "tp")),
        check_vma=False,
    )
```

```python
import functools
import math

import jax
import jax.numpy as jnp
from jax import lax
from jax.experimental import pallas as pl
from jax.experimental.pallas import tpu as pltpu
from jax.sharding import PartitionSpec as P

HEAD = 128
PAGE = 128
CTX = 8
TP = 16
SEQ = 512
HEADS = 8
GROUPS = 8
ROWS = 4
SPAN = 2048
HELP = 2
MSG = 48
F32 = jnp.float32
BF16 = jnp.bfloat16
MESH = pl.DeviceIdType.MESH
LOW = -1e30
SCALE = math.log2(math.e) / math.sqrt(HEAD)


def split_scaled(x):
    x = x.astype(F32) * SCALE
    high = x.astype(BF16)
    low = (x - high.astype(F32)).astype(BF16)
    return jnp.concatenate([high, low], axis=1)


def kernel(
    pq_ref, kt_ref, vt_ref, dq_ref, nk_ref, nv_ref, kp_ref, vp_ref, slots_ref, lens_ref, place_ref,
    out_ref, rk_ref, rv_ref, dout_ref,
    pq, qs, kv, vn, m_s, l_s, acc_s, kpool, vpool, bias, dsend, drecv, rsend, rrecv, lent, repaid, returned,
    local_sem, kv_ssem, kv_rsem, fw_ssem, fw_rsem, d_ssem, d_rsem, r_ssem, r_rsem, h_ssem, h_rsem, b_ssem, b_rsem,
):
    me = lax.axis_index("ctx")
    tp = lax.axis_index("tp")
    core = tp % 2
    mate = tp + 1 - 2 * core
    donor = me >= CTX - 2
    helper = me < 2
    partner = me ^ 6

    barrier = pltpu.get_barrier_semaphore()
    for d in range(1, CTX):
        pl.semaphore_signal(barrier, inc=1, device_id=((me + d) % CTX, tp), device_id_type=MESH)
    for d in range(1, TP):
        pl.semaphore_signal(barrier, inc=1, device_id=(me, (tp + d) % TP), device_id_type=MESH)

    load_q = pltpu.make_async_copy(pq_ref, pq, local_sem.at[0])
    load_k = pltpu.make_async_copy(kp_ref, kpool, local_sem.at[1])
    load_v = pltpu.make_async_copy(vp_ref, vpool, local_sem.at[2])
    load_q.start()
    load_k.start()
    load_v.start()

    half = pl.ds(pl.multiple_of(core * 64, 64), 64)

    def tokens(block):
        return pl.ds(pl.multiple_of(block * SEQ, SEQ), SEQ)

    kv[0, half, tokens(me)] = kt_ref[...]
    kv[1, half, tokens(me)] = vt_ref[...]

    sub = lax.broadcasted_iota(jnp.int32, (8, HEAD), 0)
    lane = lax.broadcasted_iota(jnp.int32, (8, HEAD), 1)
    first_rows = sub < 4
    for p in range(4):
        x16 = dq_ref[16 * p : 16 * p + 16, :].astype(F32)
        n16 = jnp.concatenate(
            [nk_ref[16 * p : 16 * p + 16, :], nv_ref[16 * p : 16 * p + 16, :]], axis=1
        ).astype(F32)
        for o in range(2):
            x = x16[8 * o : 8 * o + 8]
            n = n16[8 * o : 8 * o + 8]
            even, odd = [], []
            for i in range(4):
                a = x[:, 2 * i * HEAD : (2 * i + 1) * HEAD]
                b = x[:, (2 * i + 1) * HEAD : (2 * i + 2) * HEAD]
                even.append(jnp.where(first_rows, a, pltpu.roll(b, 4, 0)))
                odd.append(jnp.where(first_rows, pltpu.roll(a, 4, 0), b))
            turned = pltpu.roll(n, 4, 0)
            dsend[4 * p + 2 * o] = jnp.concatenate(even + [n, n], axis=0).astype(BF16)
            dsend[4 * p + 2 * o + 1] = jnp.concatenate(odd + [turned, turned], axis=0).astype(BF16)
    drecv[tp] = dsend[tp]

    pl.semaphore_wait(barrier, CTX + TP - 2)

    def push(block, ctx):
        return pltpu.make_async_remote_copy(
            src_ref=kv.at[:, half, tokens(block)],
            dst_ref=kv.at[:, half, tokens(block)],
            send_sem=kv_ssem.at[ctx],
            recv_sem=kv_rsem.at[block],
            device_id=(ctx, tp),
            device_id_type=MESH,
        )

    def forward(block):
        return pltpu.make_async_remote_copy(
            src_ref=kv.at[:, half, tokens(block)],
            dst_ref=kv.at[:, half, tokens(block)],
            send_sem=fw_ssem.at[block],
            recv_sem=fw_rsem.at[block],
            device_id=(me, mate),
            device_id_type=MESH,
        )

    def ask(other, slot):
        return pltpu.make_async_remote_copy(
            src_ref=dsend.at[other],
            dst_ref=drecv.at[slot],
            send_sem=d_ssem.at[other],
            recv_sem=d_rsem.at[slot],
            device_id=(me, other),
            device_id_type=MESH,
        )

    def answer(other, slot):
        return pltpu.make_async_remote_copy(
            src_ref=rsend.at[other],
            dst_ref=rrecv.at[slot],
            send_sem=r_ssem.at[other],
            recv_sem=r_rsem.at[slot],
            device_id=(me, other),
            device_id_type=MESH,
        )

    def others(do):
        def body(d, carry):
            do((tp + d) % TP)
            return carry

        lax.fori_loop(1, TP, body, 0)

    def needs(ctx, block):
        return block <= jnp.where(ctx < 2, ctx + 6, ctx)

    def lend(i):
        return pltpu.make_async_remote_copy(
            src_ref=pq.at[:, pl.ds((HEADS - HELP + i) * HEAD, HEAD)],
            dst_ref=lent.at[i],
            send_sem=h_ssem.at[i],
            recv_sem=h_rsem.at[i],
            device_id=(partner, tp),
            device_id_type=MESH,
        )

    def give_back(i):
        return pltpu.make_async_remote_copy(
            src_ref=repaid.at[i],
            dst_ref=returned.at[i],
            send_sem=b_ssem.at[i],
            recv_sem=b_rsem.at[i],
            device_id=(partner, tp),
            device_id_type=MESH,
        )

    nearest = (1, 2, 3, 6, 7, 4, 5)
    forward(me).start()
    others(lambda other: ask(other, tp).start())
    load_q.wait()

    for d in nearest:

        @pl.when(needs(me ^ d, me))
        def _(d=d):
            push(me, me ^ d).start()

    @pl.when(donor)
    def _():
        for i in range(HELP):
            lend(i).start()

    token = lax.broadcasted_iota(jnp.int32, (8, SPAN), 1)
    row = lax.broadcasted_iota(jnp.int32, (8, SPAN), 0) % ROWS
    visible = jnp.zeros((8, SPAN), F32)
    for r in range(ROWS):
        for b in range(4):
            left = jnp.minimum(lens_ref[r] - b * PAGE, PAGE)
            start = slots_ref[r, b] * PAGE
            inside = (token >= start) & (token < start + left) & (row == r)
            visible = jnp.where(inside, 1.0, visible)
    bias[...] = jnp.where(visible > 0.5, 0.0, LOW)

    for h in range(HEADS):
        qs[h] = split_scaled(pq[:, h * HEAD : (h + 1) * HEAD])

    def turn(block):
        vn[tokens(block), :] = kv[1, :, tokens(block)].T

    def unit(h, block, count, diagonal):
        width = count * SEQ
        where = pl.ds(pl.multiple_of(block * SEQ, SEQ), width)
        keys = kv[0, :, where]
        s = jnp.dot(qs[h], jnp.concatenate([keys, keys], axis=0), preferred_element_type=F32)
        if diagonal:
            query = lax.broadcasted_iota(jnp.int32, s.shape, 0)
            key = lax.broadcasted_iota(jnp.int32, s.shape, 1)
            s = jnp.where(key <= query, s, LOW)
        peak = jnp.max(s, axis=1, keepdims=True)
        if diagonal:
            peak = jnp.broadcast_to(peak, (SEQ, HEAD))
        else:
            before = m_s[h]
            peak = jnp.maximum(before, peak)
            factor = jnp.exp2(before - peak)
        m_s[h] = peak
        probs, total = [], None
        for g in range(width // HEAD):
            p = jnp.exp2(s[:, g * HEAD : (g + 1) * HEAD] - peak)
            total = p if total is None else total + p
            probs.append(p.astype(BF16))
        mixed = jnp.dot(jnp.concatenate(probs, axis=1), vn[where, :], preferred_element_type=F32)
        if diagonal:
            l_s[h] = total
            acc_s[h] = mixed
        else:
            l_s[h] = l_s[h] * factor + total
            acc_s[h] = acc_s[h] * factor + mixed

    def heads(first, last, block, count, diagonal=False):
        def body(i, carry):
            unit(2 * i, block, count, diagonal)
            unit(2 * i + 1, block, count, diagonal)
            return carry

        lax.fori_loop(first // 2, last // 2, body, 0)

    own_heads = jnp.where(donor, HEADS - HELP, HEADS)

    def take(block):
        @pl.when(needs(me, block))
        def _():
            push(block, me).wait_recv()
            forward(block).start()

    forward(me).wait_recv()
    turn(me)
    heads(0, own_heads, me, 1, diagonal=True)

    others(lambda other: ask(other, other).wait_recv())
    load_k.wait()
    load_v.wait()

    def decode_head(g):
        columns = pl.ds(pl.multiple_of(g * HEAD, HEAD), HEAD)
        mine, next_ = drecv[2 * g], drecv[2 * g + 1]
        q = jnp.concatenate([mine[:32], next_[:32]], axis=0)
        a, b = mine[32:48].astype(F32)[:8], next_[32:48].astype(F32)[:8]
        left = lane < 64
        new_k = jnp.where(left, a, pltpu.roll(b, 64, 1))
        new_v = jnp.where(left, pltpu.roll(a, 64, 1), b)
        new_k = jnp.where(first_rows, new_k, pltpu.roll(new_k, 4, 0))
        new_v = jnp.where(first_rows, new_v, pltpu.roll(new_v, 4, 0))
        s = lax.dot_general(
            q, kpool[:, columns], (((1,), (1,)), ((), ())), preferred_element_type=F32
        )
        s = (s * SCALE).reshape(8, 8, SPAN) + bias[...][None]
        own = jnp.sum(q.astype(F32).reshape(8, 8, HEAD) * new_k[None], axis=2, keepdims=True)
        own = own * SCALE
        peak = jnp.maximum(jnp.max(s, axis=2, keepdims=True), own)
        p = jnp.exp2(s - peak)
        own = jnp.exp2(own - peak)
        total = jnp.sum(p, axis=2, keepdims=True) + own
        mixed = jnp.dot(
            p.reshape(64, SPAN).astype(BF16), vpool[:, columns], preferred_element_type=F32
        ).reshape(8, 8, HEAD)
        mixed = mixed + own.astype(BF16).astype(F32) * new_v[None]
        result = (mixed / total).reshape(64, HEAD).astype(BF16)
        rsend[2 * g] = result[:32]
        rsend[2 * g + 1] = result[32:]

    def decode_two(i, carry):
        decode_head(2 * i)
        decode_head(2 * i + 1)
        return carry

    lax.fori_loop(0, GROUPS // 2, decode_two, 0)
    rrecv[tp] = rsend[tp]
    others(lambda other: answer(other, tp).start())

    for d in nearest:

        @pl.when(jnp.logical_not(needs(me ^ d, me)))
        def _(d=d):
            push(me, me ^ d).start()

    for d in (1, 2, 3):
        take(me ^ d)

    def full(block):
        @pl.when(needs(me, block))
        def _():
            forward(block).wait_recv()
            turn(block)

    full(me ^ 1)

    @pl.when(me % 2 == 1)
    def _():
        heads(0, own_heads, me - 1, 1)

    full(me ^ 2)
    full(me ^ 3)
    for d in (6, 7, 4, 5):
        take(me ^ d)

    @pl.when(me // 2 % 2 == 1)
    def _():
        heads(0, own_heads, me // 4 * 4, 2)

    for d in (6, 7, 4, 5):
        full(me ^ d)

    @pl.when(helper)
    def _():
        for i in range(HELP):
            lend(i).wait_recv()
            qs[HEADS + i] = split_scaled(lent[i])
        heads(HEADS, HEADS + HELP, partner, 1, diagonal=True)
        heads(HEADS, HEADS + HELP, 0, 4)
        heads(HEADS, HEADS + HELP, 4, 2)

        @pl.when(me == 1)
        def _():
            heads(HEADS, HEADS + HELP, 6, 1)

        for i in range(HELP):
            total = jnp.sum(l_s[HEADS + i], axis=1, keepdims=True)
            repaid[i] = (acc_s[HEADS + i] / total).astype(BF16)
            give_back(i).start()

    @pl.when(me // 4 == 1)
    def _():
        heads(0, own_heads, 0, 4)

    def normalise(h):
        total = jnp.sum(l_s[h], axis=1, keepdims=True)
        out_ref[:, h * HEAD : (h + 1) * HEAD] = (acc_s[h] / total).astype(BF16)

    for h in range(HEADS - HELP):
        normalise(h)

    @pl.when(jnp.logical_not(donor))
    def _():
        for h in range(HEADS - HELP, HEADS):
            normalise(h)

    for d in nearest:

        @pl.when(jnp.logical_not(needs(me, me ^ d)))
        def _(d=d):
            push(me ^ d, me).wait_recv()

    def relay(b, slots):
        columns = pl.ds(pl.multiple_of(b * PAGE, PAGE), PAGE)
        block = kv[:, half, columns].reshape(8, 16, PAGE)
        given = []
        for i in range(4):
            chosen = jnp.where(place_ref[b] == me * 4 + i, 1.0, 0.0)
            given.append(slots[i] + block * jnp.full((1, 16, PAGE), chosen, F32).astype(BF16))
        return tuple(given)

    empty = jnp.zeros((8, 16, PAGE), BF16)
    for i, slot in enumerate(lax.fori_loop(0, CTX * 4, relay, (empty,) * 4)):
        slot = slot.reshape(2, 64, PAGE)
        rk_ref[i] = slot[0]
        rv_ref[i] = slot[1]

    others(lambda other: answer(other, other).wait_recv())
    for p in range(4):
        pieces = []
        for o in range(2):
            even = rrecv[4 * p + 2 * o].astype(F32)
            odd = rrecv[4 * p + 2 * o + 1].astype(F32)
            columns = []
            for i in range(4):
                a, b = even[8 * i : 8 * i + 8], odd[8 * i : 8 * i + 8]
                columns.append(jnp.where(first_rows, a, pltpu.roll(b, 4, 0)))
                columns.append(jnp.where(first_rows, pltpu.roll(a, 4, 0), b))
            pieces.append(jnp.concatenate(columns, axis=1))
        dout_ref[16 * p : 16 * p + 16, :] = jnp.concatenate(pieces, axis=0).astype(BF16)

    @pl.when(donor)
    def _():
        for i in range(HELP):
            give_back(i).wait_recv()
            h = HEADS - HELP + i
            out_ref[:, h * HEAD : (h + 1) * HEAD] = returned[i]
            lend(i).wait_send()

    @pl.when(helper)
    def _():
        for i in range(HELP):
            give_back(i).wait_send()

    forward(me).wait_send()
    for d in range(1, CTX):
        push(me, me ^ d).wait_send()

        @pl.when(needs(me, me ^ d))
        def _(d=d):
            forward(me ^ d).wait_send()

    others(lambda other: ask(other, tp).wait_send())
    others(lambda other: answer(other, tp).wait_send())


def finish(*refs):
    count = (len(refs) - 1) // 3
    given, result, held = refs[:count], refs[count : 2 * count], refs[2 * count : 3 * count]
    sems = refs[-1]
    reads = [pltpu.make_async_copy(given[i], held[i], sems.at[0, i]) for i in range(count)]
    writes = [pltpu.make_async_copy(held[i], result[i], sems.at[1, i]) for i in range(count)]
    for read in reads:
        read.start()
    for read, write in zip(reads, writes):
        read.wait()
        write.start()
    for write in writes:
        write.wait()


def shards(
    prompt_queries,
    prompt_keys,
    prompt_values,
    block_slot,
    decode_queries,
    new_keys,
    new_values,
    key_pool,
    value_pool,
    slot_map,
    cache_lengths,
):
    vmem = pl.BlockSpec(memory_space=pltpu.VMEM)
    smem = pl.BlockSpec(memory_space=pltpu.SMEM)
    hbm = pl.BlockSpec(memory_space=pl.ANY)
    state = pltpu.VMEM((HEADS + HELP, SEQ, HEAD), F32)
    dma = pltpu.SemaphoreType.DMA
    shapes = (
        jax.ShapeDtypeStruct((SEQ, HEADS * HEAD), BF16),
        jax.ShapeDtypeStruct((4, 64, PAGE), BF16),
        jax.ShapeDtypeStruct((4, 64, PAGE), BF16),
        jax.ShapeDtypeStruct((64, HEADS * HEAD), BF16),
    )
    results = pl.pallas_call(
        kernel,
        out_shape=shapes,
        in_specs=[hbm, vmem, vmem, vmem, vmem, vmem, hbm, hbm, smem, smem, smem],
        out_specs=(vmem, vmem, vmem, vmem),
        scratch_shapes=[
            pltpu.VMEM((SEQ, HEADS * HEAD), BF16),
            pltpu.VMEM((HEADS + HELP, SEQ, 2 * HEAD), BF16),
            pltpu.VMEM((2, HEAD, CTX * SEQ), BF16),
            pltpu.VMEM((CTX * SEQ, HEAD), BF16),
            state,
            state,
            state,
            pltpu.VMEM((SPAN, GROUPS * HEAD), BF16),
            pltpu.VMEM((SPAN, GROUPS * HEAD), BF16),
            pltpu.VMEM((8, SPAN), F32),
            pltpu.VMEM((TP, MSG, HEAD), BF16),
            pltpu.VMEM((TP, MSG, HEAD), BF16),
            pltpu.VMEM((TP, 32, HEAD), BF16),
            pltpu.VMEM((TP, 32, HEAD), BF16),
            pltpu.VMEM((HELP, SEQ, HEAD), BF16),
            pltpu.VMEM((HELP, SEQ, HEAD), BF16),
            pltpu.VMEM((HELP, SEQ, HEAD), BF16),
            dma((3,)),
            dma((CTX,)),
            dma((CTX,)),
            dma((CTX,)),
            dma((CTX,)),
            dma((TP,)),
            dma((TP,)),
            dma((TP,)),
            dma((TP,)),
            dma((HELP,)),
            dma((HELP,)),
            dma((HELP,)),
            dma((HELP,)),
        ],
        compiler_params=pltpu.CompilerParams(
            collective_id=0, has_side_effects=True, vmem_limit_bytes=60 * 2**20
        ),
    )(
        prompt_queries,
        prompt_keys.T,
        prompt_values.T,
        decode_queries,
        new_keys,
        new_values,
        key_pool.reshape(SPAN, GROUPS * HEAD),
        value_pool.reshape(SPAN, GROUPS * HEAD),
        slot_map,
        cache_lengths,
        block_slot,
    )
    prompt_out, relaid_keys, relaid_values, decode_out = pl.pallas_call(
        finish,
        out_shape=shapes,
        in_specs=[hbm] * 4,
        out_specs=(hbm,) * 4,
        scratch_shapes=[pltpu.VMEM(one.shape, one.dtype) for one in shapes] + [dma((2, 4))],
    )(*results)
    return (
        prompt_out,
        jnp.swapaxes(relaid_keys, 1, 2),
        jnp.swapaxes(relaid_values, 1, 2),
        decode_out,
    )


def solution(mesh):
    return jax.shard_map(
        shards,
        mesh=mesh,
        in_specs=(
            P("ctx", "tp"),
            P("ctx", "tp"),
            P("ctx", "tp"),
            P(),
            P("ctx", "tp"),
            P("ctx", "tp"),
            P("ctx", "tp"),
            P(("ctx", "tp"), None, None),
            P(("ctx", "tp"), None, None),
            P(("ctx", "tp"), None),
            P(("ctx", "tp")),
        ),
        out_specs=(P("ctx", "tp"), P("ctx", None, "tp"), P("ctx", None, "tp"), P("ctx", "tp")),
        check_vma=False,
    )
```

```python
import functools
import math

import jax
import jax.numpy as jnp
from jax import lax
from jax.experimental import pallas as pl
from jax.experimental.pallas import tpu as pltpu
from jax.sharding import PartitionSpec as P

HEAD = 128
PAGE = 128
CTX = 8
TP = 16
SEQ = 512
HEADS = 8
GROUPS = 8
ROWS = 4
SPAN = 2048
HELP = 2
MSG = 48
F32 = jnp.float32
BF16 = jnp.bfloat16
MESH = pl.DeviceIdType.MESH
LOW = -1e30
SCALE = math.log2(math.e) / math.sqrt(HEAD)


def split_scaled(x):
    x = x.astype(F32) * SCALE
    high = x.astype(BF16)
    low = (x - high.astype(F32)).astype(BF16)
    return jnp.concatenate([high, low], axis=1)


def kernel(
    pq_ref, kt_in, vt_in, dq_in, nk_in, nv_in, kp_ref, vp_ref, slots_ref, lens_ref, place_ref,
    out_ref, rk_ref, rv_ref, dout_ref,
    pq, qs, kv, vn, m_s, l_s, acc_s, kpool, vpool, bias, dsend, drecv, rsend, rrecv, lent, repaid, returned, s_even, s_odd, p_even, p_odd, f_even, f_odd,
    kt_ref, vt_ref, dq_ref, nk_ref, nv_ref,
    local_sem, kv_ssem, kv_rsem, fw_ssem, fw_rsem, d_ssem, d_rsem, r_ssem, r_rsem, h_ssem, h_rsem, b_ssem, b_rsem,
):
    me = lax.axis_index("ctx")
    tp = lax.axis_index("tp")
    core = tp % 2
    mate = tp + 1 - 2 * core
    donor = me >= CTX - 2
    helper = me < 2
    partner = me ^ 6

    barrier = pltpu.get_barrier_semaphore()
    for d in range(1, CTX):
        pl.semaphore_signal(barrier, inc=1, device_id=((me + d) % CTX, tp), device_id_type=MESH)
    for d in range(1, TP):
        pl.semaphore_signal(barrier, inc=1, device_id=(me, (tp + d) % TP), device_id_type=MESH)

    pairs = ((dq_in, dq_ref), (nk_in, nk_ref), (nv_in, nv_ref), (kt_in, kt_ref), (vt_in, vt_ref))
    small = [
        pltpu.make_async_copy(given, held, local_sem.at[3 + i])
        for i, (given, held) in enumerate(pairs)
    ]
    for copy in small:
        copy.start()
    load_q = pltpu.make_async_copy(pq_ref, pq, local_sem.at[0])
    load_k = pltpu.make_async_copy(kp_ref, kpool, local_sem.at[1])
    load_v = pltpu.make_async_copy(vp_ref, vpool, local_sem.at[2])
    load_q.start()
    load_k.start()
    load_v.start()

    half = pl.ds(pl.multiple_of(core * 64, 64), 64)

    def tokens(block):
        return pl.ds(pl.multiple_of(block * SEQ, SEQ), SEQ)

    for copy in small:
        copy.wait()
    kv[0, half, tokens(me)] = kt_ref[...]
    kv[1, half, tokens(me)] = vt_ref[...]

    sub = lax.broadcasted_iota(jnp.int32, (8, HEAD), 0)
    lane = lax.broadcasted_iota(jnp.int32, (8, HEAD), 1)
    first_rows = sub < 4
    for p in range(4):
        x16 = dq_ref[16 * p : 16 * p + 16, :].astype(F32)
        n16 = jnp.concatenate(
            [nk_ref[16 * p : 16 * p + 16, :], nv_ref[16 * p : 16 * p + 16, :]], axis=1
        ).astype(F32)
        for o in range(2):
            x = x16[8 * o : 8 * o + 8]
            n = n16[8 * o : 8 * o + 8]
            even, odd = [], []
            for i in range(4):
                a = x[:, 2 * i * HEAD : (2 * i + 1) * HEAD]
                b = x[:, (2 * i + 1) * HEAD : (2 * i + 2) * HEAD]
                even.append(jnp.where(first_rows, a, pltpu.roll(b, 4, 0)))
                odd.append(jnp.where(first_rows, pltpu.roll(a, 4, 0), b))
            turned = pltpu.roll(n, 4, 0)
            dsend[4 * p + 2 * o] = jnp.concatenate(even + [n, n], axis=0).astype(BF16)
            dsend[4 * p + 2 * o + 1] = jnp.concatenate(odd + [turned, turned], axis=0).astype(BF16)
    drecv[tp] = dsend[tp]

    pl.semaphore_wait(barrier, CTX + TP - 2)

    def push(block, ctx):
        return pltpu.make_async_remote_copy(
            src_ref=kv.at[:, half, tokens(block)],
            dst_ref=kv.at[:, half, tokens(block)],
            send_sem=kv_ssem.at[ctx],
            recv_sem=kv_rsem.at[block],
            device_id=(ctx, tp),
            device_id_type=MESH,
        )

    def forward(block):
        return pltpu.make_async_remote_copy(
            src_ref=kv.at[:, half, tokens(block)],
            dst_ref=kv.at[:, half, tokens(block)],
            send_sem=fw_ssem.at[block],
            recv_sem=fw_rsem.at[block],
            device_id=(me, mate),
            device_id_type=MESH,
        )

    def ask(other, slot):
        return pltpu.make_async_remote_copy(
            src_ref=dsend.at[other],
            dst_ref=drecv.at[slot],
            send_sem=d_ssem.at[other],
            recv_sem=d_rsem.at[slot],
            device_id=(me, other),
            device_id_type=MESH,
        )

    def answer(other, slot):
        return pltpu.make_async_remote_copy(
            src_ref=rsend.at[other],
            dst_ref=rrecv.at[slot],
            send_sem=r_ssem.at[other],
            recv_sem=r_rsem.at[slot],
            device_id=(me, other),
            device_id_type=MESH,
        )

    def others(do):
        def body(d, carry):
            do((tp + d) % TP)
            return carry

        lax.fori_loop(1, TP, body, 0)

    def needs(ctx, block):
        return block <= jnp.where(ctx < 2, ctx + 6, ctx)

    def lend(i):
        return pltpu.make_async_remote_copy(
            src_ref=pq.at[:, pl.ds((HEADS - HELP + i) * HEAD, HEAD)],
            dst_ref=lent.at[i],
            send_sem=h_ssem.at[i],
            recv_sem=h_rsem.at[i],
            device_id=(partner, tp),
            device_id_type=MESH,
        )

    def give_back(i):
        return pltpu.make_async_remote_copy(
            src_ref=repaid.at[i],
            dst_ref=returned.at[i],
            send_sem=b_ssem.at[i],
            recv_sem=b_rsem.at[i],
            device_id=(partner, tp),
            device_id_type=MESH,
        )

    nearest = (1, 2, 3, 6, 7, 4, 5)
    forward(me).start()
    others(lambda other: ask(other, tp).start())
    load_q.wait()

    for d in nearest:

        @pl.when(needs(me ^ d, me))
        def _(d=d):
            push(me, me ^ d).start()

    @pl.when(donor)
    def _():
        for i in range(HELP):
            lend(i).start()

    for d in nearest:

        @pl.when(jnp.logical_not(needs(me ^ d, me)))
        def _(d=d):
            push(me, me ^ d).start()


    token = lax.broadcasted_iota(jnp.int32, (8, SPAN), 1)
    row = lax.broadcasted_iota(jnp.int32, (8, SPAN), 0) % ROWS
    visible = jnp.zeros((8, SPAN), F32)
    for r in range(ROWS):
        for b in range(4):
            left = jnp.minimum(lens_ref[r] - b * PAGE, PAGE)
            start = slots_ref[r, b] * PAGE
            inside = (token >= start) & (token < start + left) & (row == r)
            visible = jnp.where(inside, 1.0, visible)
    bias[...] = jnp.where(visible > 0.5, 0.0, LOW)

    for h in range(HEADS):
        qs[h] = split_scaled(pq[:, h * HEAD : (h + 1) * HEAD])

    def turn(block):
        vn[tokens(block), :] = kv[1, :, tokens(block)].T

    def unit(h, block, count, diagonal):
        width = count * SEQ
        where = pl.ds(pl.multiple_of(block * SEQ, SEQ), width)
        keys = kv[0, :, where]
        s = jnp.dot(qs[h], jnp.concatenate([keys, keys], axis=0), preferred_element_type=F32)
        if diagonal:
            query = lax.broadcasted_iota(jnp.int32, s.shape, 0)
            key = lax.broadcasted_iota(jnp.int32, s.shape, 1)
            s = jnp.where(key <= query, s, LOW)
        peak = jnp.max(s, axis=1, keepdims=True)
        if diagonal:
            peak = jnp.broadcast_to(peak, (SEQ, HEAD))
        else:
            before = m_s[h]
            peak = jnp.maximum(before, peak)
            factor = jnp.exp2(before - peak)
        m_s[h] = peak
        probs, total = [], None
        for g in range(width // HEAD):
            p = jnp.exp2(s[:, g * HEAD : (g + 1) * HEAD] - peak)
            total = p if total is None else total + p
            probs.append(p.astype(BF16))
        mixed = jnp.dot(jnp.concatenate(probs, axis=1), vn[where, :], preferred_element_type=F32)
        if diagonal:
            l_s[h] = total
            acc_s[h] = mixed
        else:
            l_s[h] = l_s[h] * factor + total
            acc_s[h] = acc_s[h] * factor + mixed

    def heads(first, last, block, count, diagonal=False):
        def body(i, carry):
            unit(2 * i, block, count, diagonal)
            unit(2 * i + 1, block, count, diagonal)
            return carry

        lax.fori_loop(first // 2, last // 2, body, 0)

    def scores(h, where, held):
        s_ref, peak_ref, factor_ref = held
        keys = kv[0, :, where]
        s = jnp.dot(qs[h], jnp.concatenate([keys, keys], axis=0), preferred_element_type=F32)
        s_ref[:, : where.size] = s
        before = m_s[h]
        peak = jnp.maximum(before, jnp.max(s, axis=1, keepdims=True))
        m_s[h] = peak
        peak_ref[...] = peak
        factor_ref[...] = jnp.exp2(before - peak)

    def mix(h, where, held):
        s_ref, peak_ref, factor_ref = held
        peak, factor = peak_ref[...], factor_ref[...]
        probs, total = [], None
        for g in range(where.size // HEAD):
            p = jnp.exp2(s_ref[:, g * HEAD : (g + 1) * HEAD] - peak)
            total = p if total is None else total + p
            probs.append(p.astype(BF16))
        mixed = jnp.dot(jnp.concatenate(probs, axis=1), vn[where, :], preferred_element_type=F32)
        l_s[h] = l_s[h] * factor + total
        acc_s[h] = acc_s[h] * factor + mixed

    def pipelined(first, last, block, count):
        where = pl.ds(pl.multiple_of(block * SEQ, SEQ), count * SEQ)
        even, odd = (s_even, p_even, f_even), (s_odd, p_odd, f_odd)
        scores(first, where, even)

        def body(i, carry):
            h = 2 * i
            scores(h + 1, where, odd)
            mix(h, where, even)
            scores(h + 2, where, even)
            mix(h + 1, where, odd)
            return carry

        lax.fori_loop(first // 2, last // 2 - 1, body, 0)
        scores(last - 1, where, odd)
        mix(last - 2, where, even)
        mix(last - 1, where, odd)

    own_heads = jnp.where(donor, HEADS - HELP, HEADS)

    def take(block):
        @pl.when(needs(me, block))
        def _():
            push(block, me).wait_recv()
            forward(block).start()

    forward(me).wait_recv()
    turn(me)
    heads(0, own_heads, me, 1, diagonal=True)

    others(lambda other: ask(other, other).wait_recv())
    load_k.wait()
    load_v.wait()

    def decode_head(g):
        columns = pl.ds(pl.multiple_of(g * HEAD, HEAD), HEAD)
        mine, next_ = drecv[2 * g], drecv[2 * g + 1]
        q = jnp.concatenate([mine[:32], next_[:32]], axis=0)
        a, b = mine[32:48].astype(F32)[:8], next_[32:48].astype(F32)[:8]
        left = lane < 64
        new_k = jnp.where(left, a, pltpu.roll(b, 64, 1))
        new_v = jnp.where(left, pltpu.roll(a, 64, 1), b)
        new_k = jnp.where(first_rows, new_k, pltpu.roll(new_k, 4, 0))
        new_v = jnp.where(first_rows, new_v, pltpu.roll(new_v, 4, 0))
        s = lax.dot_general(
            q, kpool[:, columns], (((1,), (1,)), ((), ())), preferred_element_type=F32
        )
        s = (s * SCALE).reshape(8, 8, SPAN) + bias[...][None]
        own = jnp.sum(q.astype(F32).reshape(8, 8, HEAD) * new_k[None], axis=2, keepdims=True)
        own = own * SCALE
        peak = jnp.maximum(jnp.max(s, axis=2, keepdims=True), own)
        p = jnp.exp2(s - peak)
        own = jnp.exp2(own - peak)
        total = jnp.sum(p, axis=2, keepdims=True) + own
        mixed = jnp.dot(
            p.reshape(64, SPAN).astype(BF16), vpool[:, columns], preferred_element_type=F32
        ).reshape(8, 8, HEAD)
        mixed = mixed + own.astype(BF16).astype(F32) * new_v[None]
        result = (mixed / total).reshape(64, HEAD).astype(BF16)
        rsend[2 * g] = result[:32]
        rsend[2 * g + 1] = result[32:]

    def decode_two(i, carry):
        decode_head(2 * i)
        decode_head(2 * i + 1)
        return carry

    lax.fori_loop(0, GROUPS // 2, decode_two, 0)
    rrecv[tp] = rsend[tp]
    others(lambda other: answer(other, tp).start())

    for d in (1, 2, 3):
        take(me ^ d)

    def full(block):
        @pl.when(needs(me, block))
        def _():
            forward(block).wait_recv()
            turn(block)

    full(me ^ 1)

    @pl.when(me % 2 == 1)
    def _():
        heads(0, own_heads, me - 1, 1)

    full(me ^ 2)
    full(me ^ 3)
    for d in (6, 7, 4, 5):
        take(me ^ d)

    @pl.when(me // 2 % 2 == 1)
    def _():
        pipelined(0, own_heads, me // 4 * 4, 2)

    for d in (6, 7, 4, 5):
        full(me ^ d)

    @pl.when(helper)
    def _():
        for i in range(HELP):
            lend(i).wait_recv()
            qs[HEADS + i] = split_scaled(lent[i])
        heads(HEADS, HEADS + HELP, partner, 1, diagonal=True)
        heads(HEADS, HEADS + HELP, 0, 4)
        heads(HEADS, HEADS + HELP, 4, 2)

        @pl.when(me == 1)
        def _():
            heads(HEADS, HEADS + HELP, 6, 1)

        for i in range(HELP):
            total = jnp.sum(l_s[HEADS + i], axis=1, keepdims=True)
            repaid[i] = (acc_s[HEADS + i] / total).astype(BF16)
            give_back(i).start()

    @pl.when(me // 4 == 1)
    def _():
        pipelined(0, own_heads, 0, 4)

    def normalise(h):
        total = jnp.sum(l_s[h], axis=1, keepdims=True)
        out_ref[:, h * HEAD : (h + 1) * HEAD] = (acc_s[h] / total).astype(BF16)

    for h in range(HEADS - HELP):
        normalise(h)

    @pl.when(jnp.logical_not(donor))
    def _():
        for h in range(HEADS - HELP, HEADS):
            normalise(h)

    for d in nearest:

        @pl.when(jnp.logical_not(needs(me, me ^ d)))
        def _(d=d):
            push(me ^ d, me).wait_recv()

    def relay(which, result):
        def body(p, carry):
            rows = pl.ds(pl.multiple_of(core * 64 + p * 16, 16), 16)
            slots = [jnp.zeros((16, PAGE), BF16)] * 4
            for b in range(CTX * 4):
                block = kv[which, rows, b * PAGE : (b + 1) * PAGE]
                for i in range(4):
                    chosen = jnp.where(place_ref[b] == me * 4 + i, 1.0, 0.0)
                    slots[i] = slots[i] + block * jnp.full((16, PAGE), chosen, F32).astype(BF16)
            for i in range(4):
                result[i, pl.ds(pl.multiple_of(p * 16, 16), 16), :] = slots[i]
            return carry

        lax.fori_loop(0, 4, body, 0)

    relay(0, rk_ref)
    relay(1, rv_ref)

    others(lambda other: answer(other, other).wait_recv())
    for p in range(4):
        pieces = []
        for o in range(2):
            even = rrecv[4 * p + 2 * o].astype(F32)
            odd = rrecv[4 * p + 2 * o + 1].astype(F32)
            columns = []
            for i in range(4):
                a, b = even[8 * i : 8 * i + 8], odd[8 * i : 8 * i + 8]
                columns.append(jnp.where(first_rows, a, pltpu.roll(b, 4, 0)))
                columns.append(jnp.where(first_rows, pltpu.roll(a, 4, 0), b))
            pieces.append(jnp.concatenate(columns, axis=1))
        dout_ref[16 * p : 16 * p + 16, :] = jnp.concatenate(pieces, axis=0).astype(BF16)

    @pl.when(donor)
    def _():
        for i in range(HELP):
            give_back(i).wait_recv()
            h = HEADS - HELP + i
            out_ref[:, h * HEAD : (h + 1) * HEAD] = returned[i]
            lend(i).wait_send()

    @pl.when(helper)
    def _():
        for i in range(HELP):
            give_back(i).wait_send()

    forward(me).wait_send()
    for d in range(1, CTX):
        push(me, me ^ d).wait_send()

        @pl.when(needs(me, me ^ d))
        def _(d=d):
            forward(me ^ d).wait_send()

    others(lambda other: ask(other, tp).wait_send())
    others(lambda other: answer(other, tp).wait_send())


def finish(*refs):
    count = (len(refs) - 1) // 2
    copies = [
        pltpu.make_async_copy(refs[i], refs[count + i], refs[-1].at[i]) for i in range(count)
    ]
    for copy in copies:
        copy.start()
    for copy in copies:
        copy.wait()


def shards(
    prompt_queries,
    prompt_keys,
    prompt_values,
    block_slot,
    decode_queries,
    new_keys,
    new_values,
    key_pool,
    value_pool,
    slot_map,
    cache_lengths,
):
    vmem = pl.BlockSpec(memory_space=pltpu.VMEM)
    smem = pl.BlockSpec(memory_space=pltpu.SMEM)
    hbm = pl.BlockSpec(memory_space=pl.ANY)
    state = pltpu.VMEM((HEADS + HELP, SEQ, HEAD), F32)
    dma = pltpu.SemaphoreType.DMA
    shapes = (
        jax.ShapeDtypeStruct((SEQ, HEADS * HEAD), BF16),
        jax.ShapeDtypeStruct((4, 64, PAGE), BF16),
        jax.ShapeDtypeStruct((4, 64, PAGE), BF16),
        jax.ShapeDtypeStruct((64, HEADS * HEAD), BF16),
    )
    results = pl.pallas_call(
        kernel,
        out_shape=tuple(pltpu.VMEM(one.shape, one.dtype) for one in shapes),
        in_specs=[hbm, hbm, hbm, hbm, hbm, hbm, hbm, hbm, smem, smem, smem],
        out_specs=(vmem, vmem, vmem, vmem),
        scratch_shapes=[
            pltpu.VMEM((SEQ, HEADS * HEAD), BF16),
            pltpu.VMEM((HEADS + HELP, SEQ, 2 * HEAD), BF16),
            pltpu.VMEM((2, HEAD, CTX * SEQ), BF16),
            pltpu.VMEM((CTX * SEQ, HEAD), BF16),
            state,
            state,
            state,
            pltpu.VMEM((SPAN, GROUPS * HEAD), BF16),
            pltpu.VMEM((SPAN, GROUPS * HEAD), BF16),
            pltpu.VMEM((8, SPAN), F32),
            pltpu.VMEM((TP, MSG, HEAD), BF16),
            pltpu.VMEM((TP, MSG, HEAD), BF16),
            pltpu.VMEM((TP, 32, HEAD), BF16),
            pltpu.VMEM((TP, 32, HEAD), BF16),
            pltpu.VMEM((HELP, SEQ, HEAD), BF16),
            pltpu.VMEM((HELP, SEQ, HEAD), BF16),
            pltpu.VMEM((HELP, SEQ, HEAD), BF16),
            pltpu.VMEM((SEQ, 4 * SEQ), F32),
            pltpu.VMEM((SEQ, 4 * SEQ), F32),
            pltpu.VMEM((SEQ, HEAD), F32),
            pltpu.VMEM((SEQ, HEAD), F32),
            pltpu.VMEM((SEQ, HEAD), F32),
            pltpu.VMEM((SEQ, HEAD), F32),
            pltpu.VMEM((64, SEQ), BF16),
            pltpu.VMEM((64, SEQ), BF16),
            pltpu.VMEM((64, HEADS * HEAD), BF16),
            pltpu.VMEM((64, 64), BF16),
            pltpu.VMEM((64, 64), BF16),
            dma((8,)),
            dma((CTX,)),
            dma((CTX,)),
            dma((CTX,)),
            dma((CTX,)),
            dma((TP,)),
            dma((TP,)),
            dma((TP,)),
            dma((TP,)),
            dma((HELP,)),
            dma((HELP,)),
            dma((HELP,)),
            dma((HELP,)),
        ],
        compiler_params=pltpu.CompilerParams(
            collective_id=0, has_side_effects=True, vmem_limit_bytes=56 * 2**20
        ),
    )(
        prompt_queries,
        prompt_keys.T,
        prompt_values.T,
        decode_queries,
        new_keys,
        new_values,
        key_pool.reshape(SPAN, GROUPS * HEAD),
        value_pool.reshape(SPAN, GROUPS * HEAD),
        slot_map,
        cache_lengths,
        block_slot,
    )
    prompt_out, relaid_keys, relaid_values, decode_out = pl.pallas_call(
        finish,
        out_shape=shapes,
        in_specs=[vmem] * 4,
        out_specs=(hbm,) * 4,
        scratch_shapes=[dma((4,))],
    )(*[pltpu.with_memory_space_constraint(one, pltpu.VMEM) for one in results])
    return (
        prompt_out,
        jnp.swapaxes(relaid_keys, 1, 2),
        jnp.swapaxes(relaid_values, 1, 2),
        decode_out,
    )


def solution(mesh):
    return jax.shard_map(
        shards,
        mesh=mesh,
        in_specs=(
            P("ctx", "tp"),
            P("ctx", "tp"),
            P("ctx", "tp"),
            P(),
            P("ctx", "tp"),
            P("ctx", "tp"),
            P("ctx", "tp"),
            P(("ctx", "tp"), None, None),
            P(("ctx", "tp"), None, None),
            P(("ctx", "tp"), None),
            P(("ctx", "tp")),
        ),
        out_specs=(P("ctx", "tp"), P("ctx", None, "tp"), P("ctx", None, "tp"), P("ctx", "tp")),
        check_vma=False,
    )
```

```python
import functools
import math

import jax
import jax.numpy as jnp
from jax import lax
from jax.experimental import pallas as pl
from jax.experimental.pallas import tpu as pltpu
from jax.sharding import PartitionSpec as P

HEAD = 128
PAGE = 128
CTX = 8
TP = 16
SEQ = 512
HEADS = 8
GROUPS = 8
ROWS = 4
SPAN = 2048
HELP = 2
MSG = 48
F32 = jnp.float32
BF16 = jnp.bfloat16
MESH = pl.DeviceIdType.MESH
LOW = -1e30
SCALE = math.log2(math.e) / math.sqrt(HEAD)


def split_scaled(x):
    x = x.astype(F32) * SCALE
    high = x.astype(BF16)
    low = (x - high.astype(F32)).astype(BF16)
    return jnp.concatenate([high, low], axis=1)


def kernel(
    pq_ref, kt_in, vt_in, dq_in, nk_in, nv_in, kp_ref, vp_ref, slots_ref, lens_ref, place_ref,
    out_ref, rk_ref, rv_ref, dout_ref,
    pq, qs, kv, vn, m_s, l_s, acc_s, kpool, vpool, bias, dsend, drecv, rsend, rrecv, lent, repaid, returned, s_even, s_odd, p_even, p_odd, f_even, f_odd,
    kt_ref, vt_ref, dq_ref, nk_ref, nv_ref,
    local_sem, kv_ssem, kv_rsem, fw_ssem, fw_rsem, d_ssem, d_rsem, r_ssem, r_rsem, h_ssem, h_rsem, b_ssem, b_rsem,
):
    me = lax.axis_index("ctx")
    tp = lax.axis_index("tp")
    core = tp % 2
    mate = tp + 1 - 2 * core
    donor = me >= CTX - 2
    helper = me < 2
    partner = me ^ 6

    barrier = pltpu.get_barrier_semaphore()
    for d in range(1, CTX):
        pl.semaphore_signal(barrier, inc=1, device_id=((me + d) % CTX, tp), device_id_type=MESH)
    for d in range(1, TP):
        pl.semaphore_signal(barrier, inc=1, device_id=(me, (tp + d) % TP), device_id_type=MESH)

    pairs = ((dq_in, dq_ref), (nk_in, nk_ref), (nv_in, nv_ref), (kt_in, kt_ref), (vt_in, vt_ref))
    small = [
        pltpu.make_async_copy(given, held, local_sem.at[3 + i])
        for i, (given, held) in enumerate(pairs)
    ]
    for copy in small:
        copy.start()
    load_q = pltpu.make_async_copy(pq_ref, pq, local_sem.at[0])
    load_k = pltpu.make_async_copy(kp_ref, kpool, local_sem.at[1])
    load_v = pltpu.make_async_copy(vp_ref, vpool, local_sem.at[2])
    load_q.start()
    load_k.start()
    load_v.start()

    half = pl.ds(pl.multiple_of(core * 64, 64), 64)

    def tokens(block):
        return pl.ds(pl.multiple_of(block * SEQ, SEQ), SEQ)

    for copy in small:
        copy.wait()
    kv[0, half, tokens(me)] = kt_ref[...]
    kv[1, half, tokens(me)] = vt_ref[...]

    sub = lax.broadcasted_iota(jnp.int32, (8, HEAD), 0)
    lane = lax.broadcasted_iota(jnp.int32, (8, HEAD), 1)
    first_rows = sub < 4
    for p in range(4):
        x16 = dq_ref[16 * p : 16 * p + 16, :].astype(F32)
        n16 = jnp.concatenate(
            [nk_ref[16 * p : 16 * p + 16, :], nv_ref[16 * p : 16 * p + 16, :]], axis=1
        ).astype(F32)
        for o in range(2):
            x = x16[8 * o : 8 * o + 8]
            n = n16[8 * o : 8 * o + 8]
            even, odd = [], []
            for i in range(4):
                a = x[:, 2 * i * HEAD : (2 * i + 1) * HEAD]
                b = x[:, (2 * i + 1) * HEAD : (2 * i + 2) * HEAD]
                even.append(jnp.where(first_rows, a, pltpu.roll(b, 4, 0)))
                odd.append(jnp.where(first_rows, pltpu.roll(a, 4, 0), b))
            turned = pltpu.roll(n, 4, 0)
            dsend[4 * p + 2 * o] = jnp.concatenate(even + [n, n], axis=0).astype(BF16)
            dsend[4 * p + 2 * o + 1] = jnp.concatenate(odd + [turned, turned], axis=0).astype(BF16)
    drecv[tp] = dsend[tp]

    pl.semaphore_wait(barrier, CTX + TP - 2)

    def push(block, ctx):
        return pltpu.make_async_remote_copy(
            src_ref=kv.at[:, half, tokens(block)],
            dst_ref=kv.at[:, half, tokens(block)],
            send_sem=kv_ssem.at[ctx],
            recv_sem=kv_rsem.at[block],
            device_id=(ctx, tp),
            device_id_type=MESH,
        )

    def forward(block):
        return pltpu.make_async_remote_copy(
            src_ref=kv.at[:, half, tokens(block)],
            dst_ref=kv.at[:, half, tokens(block)],
            send_sem=fw_ssem.at[block],
            recv_sem=fw_rsem.at[block],
            device_id=(me, mate),
            device_id_type=MESH,
        )

    def ask(other, slot):
        return pltpu.make_async_remote_copy(
            src_ref=dsend.at[other],
            dst_ref=drecv.at[slot],
            send_sem=d_ssem.at[other],
            recv_sem=d_rsem.at[slot],
            device_id=(me, other),
            device_id_type=MESH,
        )

    def answer(other, slot):
        return pltpu.make_async_remote_copy(
            src_ref=rsend.at[other],
            dst_ref=rrecv.at[slot],
            send_sem=r_ssem.at[other],
            recv_sem=r_rsem.at[slot],
            device_id=(me, other),
            device_id_type=MESH,
        )

    def others(do):
        def body(d, carry):
            do((tp + d) % TP)
            return carry

        lax.fori_loop(1, TP, body, 0)

    def needs(ctx, block):
        return block <= jnp.where(ctx < 2, ctx + 6, ctx)

    def lend(i):
        return pltpu.make_async_remote_copy(
            src_ref=pq.at[:, pl.ds((HEADS - HELP + i) * HEAD, HEAD)],
            dst_ref=lent.at[i],
            send_sem=h_ssem.at[i],
            recv_sem=h_rsem.at[i],
            device_id=(partner, tp),
            device_id_type=MESH,
        )

    def give_back(i):
        return pltpu.make_async_remote_copy(
            src_ref=repaid.at[i],
            dst_ref=returned.at[i],
            send_sem=b_ssem.at[i],
            recv_sem=b_rsem.at[i],
            device_id=(partner, tp),
            device_id_type=MESH,
        )

    nearest = (1, 2, 3, 6, 7, 4, 5)
    forward(me).start()
    others(lambda other: ask(other, tp).start())
    load_q.wait()

    for d in nearest:

        @pl.when(needs(me ^ d, me))
        def _(d=d):
            push(me, me ^ d).start()

    @pl.when(donor)
    def _():
        for i in range(HELP):
            lend(i).start()

    for d in nearest:

        @pl.when(jnp.logical_not(needs(me ^ d, me)))
        def _(d=d):
            push(me, me ^ d).start()


    token = lax.broadcasted_iota(jnp.int32, (8, SPAN), 1)
    row = lax.broadcasted_iota(jnp.int32, (8, SPAN), 0) % ROWS
    visible = jnp.zeros((8, SPAN), F32)
    for r in range(ROWS):
        for b in range(4):
            left = jnp.minimum(lens_ref[r] - b * PAGE, PAGE)
            start = slots_ref[r, b] * PAGE
            inside = (token >= start) & (token < start + left) & (row == r)
            visible = jnp.where(inside, 1.0, visible)
    bias[...] = jnp.where(visible > 0.5, 0.0, LOW)

    for h in range(HEADS):
        qs[h] = split_scaled(pq[:, h * HEAD : (h + 1) * HEAD])

    def turn(block):
        vn[tokens(block), :] = kv[1, :, tokens(block)].T

    def unit(h, block, count, diagonal):
        width = count * SEQ
        where = pl.ds(pl.multiple_of(block * SEQ, SEQ), width)
        keys = kv[0, :, where]
        s = jnp.dot(qs[h], jnp.concatenate([keys, keys], axis=0), preferred_element_type=F32)
        if diagonal:
            query = lax.broadcasted_iota(jnp.int32, s.shape, 0)
            key = lax.broadcasted_iota(jnp.int32, s.shape, 1)
            s = jnp.where(key <= query, s, LOW)
        peak = jnp.max(s, axis=1, keepdims=True)
        if diagonal:
            peak = jnp.broadcast_to(peak, (SEQ, HEAD))
        else:
            before = m_s[h]
            peak = jnp.maximum(before, peak)
            factor = jnp.exp2(before - peak)
        m_s[h] = peak
        probs, total = [], None
        for g in range(width // HEAD):
            p = jnp.exp2(s[:, g * HEAD : (g + 1) * HEAD] - peak)
            total = p if total is None else total + p
            probs.append(p.astype(BF16))
        mixed = jnp.dot(jnp.concatenate(probs, axis=1), vn[where, :], preferred_element_type=F32)
        if diagonal:
            l_s[h] = total
            acc_s[h] = mixed
        else:
            l_s[h] = l_s[h] * factor + total
            acc_s[h] = acc_s[h] * factor + mixed

    def heads(first, last, block, count, diagonal=False):
        def body(i, carry):
            unit(2 * i, block, count, diagonal)
            unit(2 * i + 1, block, count, diagonal)
            return carry

        lax.fori_loop(first // 2, last // 2, body, 0)

    def scores(h, where, held):
        s_ref, peak_ref, factor_ref = held
        keys = kv[0, :, where]
        s = jnp.dot(qs[h], jnp.concatenate([keys, keys], axis=0), preferred_element_type=F32)
        s_ref[:, : where.size] = s
        before = m_s[h]
        peak = jnp.maximum(before, jnp.max(s, axis=1, keepdims=True))
        m_s[h] = peak
        peak_ref[...] = peak
        factor_ref[...] = jnp.exp2(before - peak)

    def mix(h, where, held):
        s_ref, peak_ref, factor_ref = held
        peak, factor = peak_ref[...], factor_ref[...]
        probs, total = [], None
        for g in range(where.size // HEAD):
            p = jnp.exp2(s_ref[:, g * HEAD : (g + 1) * HEAD] - peak)
            total = p if total is None else total + p
            probs.append(p.astype(BF16))
        mixed = jnp.dot(jnp.concatenate(probs, axis=1), vn[where, :], preferred_element_type=F32)
        l_s[h] = l_s[h] * factor + total
        acc_s[h] = acc_s[h] * factor + mixed

    def pipelined(first, last, block, count):
        where = pl.ds(pl.multiple_of(block * SEQ, SEQ), count * SEQ)
        even, odd = (s_even, p_even, f_even), (s_odd, p_odd, f_odd)
        scores(first, where, even)

        def body(i, carry):
            h = 2 * i
            scores(h + 1, where, odd)
            mix(h, where, even)
            scores(h + 2, where, even)
            mix(h + 1, where, odd)
            return carry

        lax.fori_loop(first // 2, last // 2 - 1, body, 0)
        scores(last - 1, where, odd)
        mix(last - 2, where, even)
        mix(last - 1, where, odd)

    own_heads = jnp.where(donor, HEADS - HELP, HEADS)

    def take(block):
        @pl.when(needs(me, block))
        def _():
            push(block, me).wait_recv()
            forward(block).start()

    forward(me).wait_recv()
    turn(me)
    heads(0, own_heads, me, 1, diagonal=True)

    others(lambda other: ask(other, other).wait_recv())
    load_k.wait()
    load_v.wait()

    def decode_head(g):
        columns = pl.ds(pl.multiple_of(g * HEAD, HEAD), HEAD)
        mine, next_ = drecv[2 * g], drecv[2 * g + 1]
        q = jnp.concatenate([mine[:32], next_[:32]], axis=0)
        a, b = mine[32:48].astype(F32)[:8], next_[32:48].astype(F32)[:8]
        left = lane < 64
        new_k = jnp.where(left, a, pltpu.roll(b, 64, 1))
        new_v = jnp.where(left, pltpu.roll(a, 64, 1), b)
        new_k = jnp.where(first_rows, new_k, pltpu.roll(new_k, 4, 0))
        new_v = jnp.where(first_rows, new_v, pltpu.roll(new_v, 4, 0))
        s = lax.dot_general(
            q, kpool[:, columns], (((1,), (1,)), ((), ())), preferred_element_type=F32
        )
        s = (s * SCALE).reshape(8, 8, SPAN) + bias[...][None]
        own = jnp.sum(q.astype(F32).reshape(8, 8, HEAD) * new_k[None], axis=2, keepdims=True)
        own = own * SCALE
        peak = jnp.maximum(jnp.max(s, axis=2, keepdims=True), own)
        p = jnp.exp2(s - peak)
        own = jnp.exp2(own - peak)
        total = jnp.sum(p, axis=2, keepdims=True) + own
        mixed = jnp.dot(
            p.reshape(64, SPAN).astype(BF16), vpool[:, columns], preferred_element_type=F32
        ).reshape(8, 8, HEAD)
        mixed = mixed + own.astype(BF16).astype(F32) * new_v[None]
        result = (mixed / total).reshape(64, HEAD).astype(BF16)
        rsend[2 * g] = result[:32]
        rsend[2 * g + 1] = result[32:]

    def decode_two(i, carry):
        decode_head(2 * i)
        decode_head(2 * i + 1)
        return carry

    lax.fori_loop(0, GROUPS // 2, decode_two, 0)
    rrecv[tp] = rsend[tp]
    others(lambda other: answer(other, tp).start())

    for d in (1, 2, 3):
        take(me ^ d)

    def full(block):
        @pl.when(needs(me, block))
        def _():
            forward(block).wait_recv()
            turn(block)

    full(me ^ 1)

    @pl.when(me % 2 == 1)
    def _():
        heads(0, own_heads, me - 1, 1)

    full(me ^ 2)
    full(me ^ 3)
    for d in (6, 7, 4, 5):
        take(me ^ d)

    @pl.when(me // 2 % 2 == 1)
    def _():
        pipelined(0, own_heads, me // 4 * 4, 2)

    for d in (6, 7, 4, 5):
        full(me ^ d)

    @pl.when(helper)
    def _():
        for i in range(HELP):
            lend(i).wait_recv()
            qs[HEADS + i] = split_scaled(lent[i])

        def help_with(i, carry):
            h = HEADS + i
            unit(h, partner, 1, True)
            unit(h, 0, 4, False)
            unit(h, 4, 2, False)

            @pl.when(me == 1)
            def _():
                unit(h, 6, 1, False)

            total = jnp.sum(l_s[h], axis=1, keepdims=True)
            repaid[i] = (acc_s[h] / total).astype(BF16)
            give_back(i).start()
            return carry

        lax.fori_loop(0, HELP, help_with, 0)

    @pl.when(me // 4 == 1)
    def _():
        pipelined(0, own_heads, 0, 4)

    def normalise(h):
        total = jnp.sum(l_s[h], axis=1, keepdims=True)
        out_ref[:, h * HEAD : (h + 1) * HEAD] = (acc_s[h] / total).astype(BF16)

    for h in range(HEADS - HELP):
        normalise(h)

    @pl.when(jnp.logical_not(donor))
    def _():
        for h in range(HEADS - HELP, HEADS):
            normalise(h)

    for d in nearest:

        @pl.when(jnp.logical_not(needs(me, me ^ d)))
        def _(d=d):
            push(me ^ d, me).wait_recv()

    def relay(which, result):
        def body(p, carry):
            rows = pl.ds(pl.multiple_of(core * 64 + p * 16, 16), 16)
            slots = [jnp.zeros((16, PAGE), BF16)] * 4
            for b in range(CTX * 4):
                block = kv[which, rows, b * PAGE : (b + 1) * PAGE]
                for i in range(4):
                    chosen = jnp.where(place_ref[b] == me * 4 + i, 1.0, 0.0)
                    slots[i] = slots[i] + block * jnp.full((16, PAGE), chosen, F32).astype(BF16)
            for i in range(4):
                result[i, pl.ds(pl.multiple_of(p * 16, 16), 16), :] = slots[i]
            return carry

        lax.fori_loop(0, 4, body, 0)

    relay(0, rk_ref)
    relay(1, rv_ref)

    others(lambda other: answer(other, other).wait_recv())
    for p in range(4):
        pieces = []
        for o in range(2):
            even = rrecv[4 * p + 2 * o].astype(F32)
            odd = rrecv[4 * p + 2 * o + 1].astype(F32)
            columns = []
            for i in range(4):
                a, b = even[8 * i : 8 * i + 8], odd[8 * i : 8 * i + 8]
                columns.append(jnp.where(first_rows, a, pltpu.roll(b, 4, 0)))
                columns.append(jnp.where(first_rows, pltpu.roll(a, 4, 0), b))
            pieces.append(jnp.concatenate(columns, axis=1))
        dout_ref[16 * p : 16 * p + 16, :] = jnp.concatenate(pieces, axis=0).astype(BF16)

    @pl.when(donor)
    def _():
        for i in range(HELP):
            give_back(i).wait_recv()
            h = HEADS - HELP + i
            out_ref[:, h * HEAD : (h + 1) * HEAD] = returned[i]
            lend(i).wait_send()

    @pl.when(helper)
    def _():
        for i in range(HELP):
            give_back(i).wait_send()

    forward(me).wait_send()
    for d in range(1, CTX):
        push(me, me ^ d).wait_send()

        @pl.when(needs(me, me ^ d))
        def _(d=d):
            forward(me ^ d).wait_send()

    others(lambda other: ask(other, tp).wait_send())
    others(lambda other: answer(other, tp).wait_send())


def finish(*refs):
    count = (len(refs) - 1) // 2
    copies = [
        pltpu.make_async_copy(refs[i], refs[count + i], refs[-1].at[i]) for i in range(count)
    ]
    for copy in copies:
        copy.start()
    for copy in copies:
        copy.wait()


def shards(
    prompt_queries,
    prompt_keys,
    prompt_values,
    block_slot,
    decode_queries,
    new_keys,
    new_values,
    key_pool,
    value_pool,
    slot_map,
    cache_lengths,
):
    vmem = pl.BlockSpec(memory_space=pltpu.VMEM)
    smem = pl.BlockSpec(memory_space=pltpu.SMEM)
    hbm = pl.BlockSpec(memory_space=pl.ANY)
    state = pltpu.VMEM((HEADS + HELP, SEQ, HEAD), F32)
    dma = pltpu.SemaphoreType.DMA
    shapes = (
        jax.ShapeDtypeStruct((SEQ, HEADS * HEAD), BF16),
        jax.ShapeDtypeStruct((4, 64, PAGE), BF16),
        jax.ShapeDtypeStruct((4, 64, PAGE), BF16),
        jax.ShapeDtypeStruct((64, HEADS * HEAD), BF16),
    )
    results = pl.pallas_call(
        kernel,
        out_shape=tuple(pltpu.VMEM(one.shape, one.dtype) for one in shapes),
        in_specs=[hbm, hbm, hbm, hbm, hbm, hbm, hbm, hbm, smem, smem, smem],
        out_specs=(vmem, vmem, vmem, vmem),
        scratch_shapes=[
            pltpu.VMEM((SEQ, HEADS * HEAD), BF16),
            pltpu.VMEM((HEADS + HELP, SEQ, 2 * HEAD), BF16),
            pltpu.VMEM((2, HEAD, CTX * SEQ), BF16),
            pltpu.VMEM((CTX * SEQ, HEAD), BF16),
            state,
            state,
            state,
            pltpu.VMEM((SPAN, GROUPS * HEAD), BF16),
            pltpu.VMEM((SPAN, GROUPS * HEAD), BF16),
            pltpu.VMEM((8, SPAN), F32),
            pltpu.VMEM((TP, MSG, HEAD), BF16),
            pltpu.VMEM((TP, MSG, HEAD), BF16),
            pltpu.VMEM((TP, 32, HEAD), BF16),
            pltpu.VMEM((TP, 32, HEAD), BF16),
            pltpu.VMEM((HELP, SEQ, HEAD), BF16),
            pltpu.VMEM((HELP, SEQ, HEAD), BF16),
            pltpu.VMEM((HELP, SEQ, HEAD), BF16),
            pltpu.VMEM((SEQ, 4 * SEQ), F32),
            pltpu.VMEM((SEQ, 4 * SEQ), F32),
            pltpu.VMEM((SEQ, HEAD), F32),
            pltpu.VMEM((SEQ, HEAD), F32),
            pltpu.VMEM((SEQ, HEAD), F32),
            pltpu.VMEM((SEQ, HEAD), F32),
            pltpu.VMEM((64, SEQ), BF16),
            pltpu.VMEM((64, SEQ), BF16),
            pltpu.VMEM((64, HEADS * HEAD), BF16),
            pltpu.VMEM((64, 64), BF16),
            pltpu.VMEM((64, 64), BF16),
            dma((8,)),
            dma((CTX,)),
            dma((CTX,)),
            dma((CTX,)),
            dma((CTX,)),
            dma((TP,)),
            dma((TP,)),
            dma((TP,)),
            dma((TP,)),
            dma((HELP,)),
            dma((HELP,)),
            dma((HELP,)),
            dma((HELP,)),
        ],
        compiler_params=pltpu.CompilerParams(
            collective_id=0, has_side_effects=True, vmem_limit_bytes=56 * 2**20
        ),
    )(
        prompt_queries,
        prompt_keys.T,
        prompt_values.T,
        decode_queries,
        new_keys,
        new_values,
        key_pool.reshape(SPAN, GROUPS * HEAD),
        value_pool.reshape(SPAN, GROUPS * HEAD),
        slot_map,
        cache_lengths,
        block_slot,
    )
    prompt_out, relaid_keys, relaid_values, decode_out = pl.pallas_call(
        finish,
        out_shape=shapes,
        in_specs=[vmem] * 4,
        out_specs=(hbm,) * 4,
        scratch_shapes=[dma((4,))],
    )(*[pltpu.with_memory_space_constraint(one, pltpu.VMEM) for one in results])
    return (
        prompt_out,
        jnp.swapaxes(relaid_keys, 1, 2),
        jnp.swapaxes(relaid_values, 1, 2),
        decode_out,
    )


def solution(mesh):
    return jax.shard_map(
        shards,
        mesh=mesh,
        in_specs=(
            P("ctx", "tp"),
            P("ctx", "tp"),
            P("ctx", "tp"),
            P(),
            P("ctx", "tp"),
            P("ctx", "tp"),
            P("ctx", "tp"),
            P(("ctx", "tp"), None, None),
            P(("ctx", "tp"), None, None),
            P(("ctx", "tp"), None),
            P(("ctx", "tp")),
        ),
        out_specs=(P("ctx", "tp"), P("ctx", None, "tp"), P("ctx", None, "tp"), P("ctx", "tp")),
        check_vma=False,
    )
```
